32 devices in a mesh: front: 2 (over x), row: 4 (over y, core), col: 4 (over z).
Axes of the slice: x: 2, y: 2, z: 4, core: 2. Of those that a mesh axis runs over, the one named last changes fastest.
Arguments:
- parent: bfloat16 [49152, 1024], P(('front', 'row'), 'col'), parts along dimension 0, may hold values from -6 to 6
- contrib: bfloat16 [896, 256, 256], P(('front', 'row', 'col')), parts along dimension 0, may hold values from -6 to 6
- owner: int32 [896, 1], P(('front', 'row', 'col')), parts along dimension 0, may hold values from 0 to 15; in each aligned block of 28 rows (0 to 27, 28 to 55, ...) at most 2 rows name the same one
- slot: int32 [896], P(('front', 'row', 'col')), parts along dimension 0, may hold values from 0 to 23
- pivot: float32 [512, 256], P(('front', 'row', 'col')), parts along dimension 0, as said below
- u_factor: bfloat16 [49152, 64], P(('front', 'row', 'col')), parts along dimension 0, may hold values from -1.5 to 1.5
- v_factor: bfloat16 [49152, 64], P(('front', 'row', 'col')), parts along dimension 0, may hold values from -6 to 6
- rank: int32 [192], P(('front', 'row', 'col')), parts along dimension 0, may hold values from 8 to 64
Outputs:
- schur: float32 [49152, 1024], P(('front', 'row'), 'col'), parts along dimension 0
The draws below stay inside these ranges and needn't reach their ends.
There are 2 independent parts, one for each index of `front`. The reference program is written for one: setup_inputs(seed, part) draws one part's arguments, and reference() takes and returns one part's arrays. A program takes and returns all parts, laid end to end along the dimension named above; each array names one. Nothing has to cross between parts.
Inputs may be any that keep to these rules, and one draw needn't show every extreme that they name: Among the 28 blocks of one device at most 2 name one owner, a bound that some block reaches. `pivot`: Symmetric; each diagonal entry exceeds the sum of the magnitudes of the other entries of its row.
All inputs are finite; a program needn't handle non-finite values.
Results may differ from the reference program's by a relative error of at most 0.0005.
Values may be sent and summed in bfloat16 or wider, within the bound.
A program may use at most 128 MiB of HBM per device.

```python
import math
import jax
import jax.numpy as jnp
import numpy as np
from jax import lax

B = 256
NR = 96
RMAX = 64
KB = 28
CAP = 2
WC_DEV = 1
LOC = 24
WCOLS = 4
CONTRIBS = 448
N_ROW = 4
N_COL = 4


def draw_pivot(key, part):
    key = jax.random.fold_in(key, 7)
    first, second = jax.random.split(key)
    raw = jax.random.uniform(first, (B, B), jnp.float32, -1.0, 1.0)
    off = (raw + raw.T) * (8.0 / B)
    off = off * (1.0 - jnp.eye(B, dtype=jnp.float32))
    diag = 20.0 + 10.0 * jax.random.uniform(second, (B,), jnp.float32)
    return off + jnp.diag(diag)


def plant(values, rng, least, high):
    longest = values.shape.index(max(values.shape))
    spots = []
    for shift in (0, 1):
        where = [jax.random.randint(jax.random.fold_in(rng, axis), (), 0, length) for axis, length in enumerate(values.shape)]
        where[longest] = (where[longest] + shift) % values.shape[longest]
        spots.append(tuple(where))
    return values.at[spots[0]].set(least).at[spots[1]].set(high)


def block_scale(stream_key, dims, cuts, smallest, high):
    gain, own = 1.0, jax.random.fold_in(stream_key, 6)
    for dim, shards_of in cuts:
        heights = jnp.exp(jax.random.uniform(jax.random.fold_in(own, dim), (shards_of,), jnp.float32, smallest / len(cuts), high / len(cuts)))
        gain = gain * jnp.repeat(heights, dims[dim] // shards_of).reshape([-1 if axis == dim else 1 for axis in range(len(dims))])
    return gain


def routed_block(key, own, number, rows, amount, top, reach, lean):
    sequence = jax.random.permutation(key, amount)
    heavy_load, ordinary = shares(amount, rows * top, reach, lean, True), shares(amount, rows * top, reach, lean, False)
    places = jnp.arange(amount)

    def named(tallies, offset_by):
        used = int((tallies > 0).sum())
        fixed = max(1, used // 4)
        shifted = fixed + (places - fixed + offset_by * (used - fixed)) % max(1, amount - fixed)
        return jnp.zeros((amount,), jnp.int32).at[sequence[jnp.where(places < fixed, places, shifted)]].set(jnp.asarray(tallies, jnp.int32))

    tallies = jnp.where(number % 4 == 0, named(heavy_load, number // 4), named(ordinary, number - number // 4 - 1))
    mixed = jax.random.permutation(jax.random.fold_in(own, 3), amount)
    source_of, receiver = mixed[0:amount // 2 * 2:2], mixed[1:amount // 2 * 2:2]
    margin = jnp.minimum(tallies[source_of] - 1, reach - tallies[receiver]) // 2
    margin = jnp.where((source_of == sequence[0]) | (receiver == sequence[0]) | (tallies[receiver] == 0), 0, jnp.maximum(margin, 0))
    shifted = jax.random.randint(jax.random.fold_in(own, 4), (amount // 2,), 0, 1 << 20) % (margin + 1)
    tallies = tallies.at[source_of].add(-shifted).at[receiver].add(shifted)
    members = jnp.searchsorted(jnp.cumsum(tallies), jnp.arange(rows * top), side="right").astype(jnp.int32)
    table = members.reshape(top, rows).T
    table = table[jax.random.permutation(jax.random.fold_in(own, 1), rows)]
    offset_by = jax.random.randint(jax.random.fold_in(own, 2), (rows, 1), 0, top)
    return jnp.take_along_axis(table, (jnp.arange(top)[None, :] + offset_by) % top, axis=1)


def shares(amount, total, limit, skew, full):
    weights = [(1 << 20) // math.isqrt(standing ** skew) + 1 for standing in range(1, amount + 1)]
    largest = limit if full else min(limit, max(-(-total // amount), total * weights[0] // sum(weights)))
    least = 1 if total - largest >= amount - 1 else 0
    given, rest = [largest] + [least] * (amount - 1), total - largest - least * (amount - 1)
    while rest > 0:
        movable = [i for i in range(1, amount) if given[i] < largest] or [i for i in range(1, amount) if given[i] < limit]
        pool, remaining = sum([weights[i] for i in movable]), rest
        for i in movable:
            extra = min(limit - given[i], max(1, remaining * weights[i] // pool), rest)
            given[i] = given[i] + extra
            rest = rest - extra
    return np.array(given)


def normal_values(stream_key, dims, deviation, most, pieces=(), held_as=jnp.bfloat16):
    entries = deviation * jax.random.normal(stream_key, dims, jnp.float32)
    if pieces:
        entries = entries * block_scale(stream_key, dims, pieces, -0.22, 0.18)
    return jnp.clip(entries, -most, most).astype(held_as)


def setup_inputs(seed: int = 0, part: int = 0) -> dict:
    arg_keys = jax.random.split(jax.random.key(seed), 9)
    own_keys = jax.random.split(jax.random.fold_in(arg_keys[8], part), 9)
    parent = normal_values(own_keys[0], (NR * B, WCOLS * B), 1.0, 6.0, ((0, 4), (1, 4)))
    contrib = normal_values(own_keys[1], (CONTRIBS, B, B), 1.0, 6.0, ((0, 16),))
    owner_keys = jax.random.split(jax.random.fold_in(own_keys[2], 1), CONTRIBS // KB)
    owner_turns = jax.random.permutation(jax.random.fold_in(own_keys[2], 3), CONTRIBS // KB)
    owner = jax.vmap(lambda own, number: routed_block(jax.random.fold_in(own_keys[2], 2), own, number, KB, N_ROW * N_COL, 1, CAP, 2))(owner_keys, owner_turns).reshape((CONTRIBS, 1))
    slot = plant(jax.random.randint(own_keys[3], (CONTRIBS,), 0, LOC), jax.random.fold_in(own_keys[3], 1), 0, LOC - 1).astype(jnp.int32)
    pivot = draw_pivot(jax.random.fold_in(jax.random.fold_in(arg_keys[8], part), 71), part)
    u_factor = normal_values(own_keys[5], (NR * B, RMAX), 0.25, 1.5, ((0, 16),))
    v_factor = normal_values(own_keys[6], (NR * B, RMAX), 1.0, 6.0, ((0, 16),))
    rank = plant(jax.random.randint(own_keys[7], (NR,), RMAX // 8, RMAX + 1), jax.random.fold_in(own_keys[7], 1), RMAX // 8, RMAX).astype(jnp.int32)
    return dict(parent=parent, contrib=contrib, owner=owner, slot=slot, pivot=pivot, u_factor=u_factor, v_factor=v_factor, rank=rank)


def schur_complement_term(u_rows, g_rows, upper_columns, g_cols):
    middle = jnp.einsum('nbr,tbs->ntrs', g_rows.astype(jnp.float32), g_cols.astype(jnp.float32)).astype(jnp.bfloat16)
    left_operand = jnp.einsum('nbr,ntrs->ntbs', u_rows.astype(jnp.float32), middle.astype(jnp.float32)).astype(jnp.bfloat16)
    update_term = jnp.einsum('rufe,ude->rfud', left_operand.astype(jnp.float32), upper_columns.astype(jnp.float32))
    return update_term.reshape(u_rows.shape[0] * B, upper_columns.shape[0] * B)

def reference(parent, contrib, owner, slot, pivot, u_factor, v_factor, rank):
    devices = N_ROW * N_COL
    row_block_list = NR // N_ROW
    per_dev = NR // devices
    wcols = WC_DEV * N_COL
    target = owner[:, 0]
    grow = target // N_COL * row_block_list + slot // WC_DEV
    gcol = target % N_COL * WC_DEV + slot % WC_DEV
    where_to = (grow * wcols + gcol).astype(jnp.int32)
    added = jax.ops.segment_sum(contrib.astype(jnp.float32).reshape(-1, B * B), where_to, num_segments=NR * wcols)
    added = added.reshape(NR, wcols, B, B).transpose(0, 2, 1, 3).reshape(NR * B, wcols * B)
    summed = parent.astype(jnp.float32) + added
    lower = jnp.linalg.cholesky(pivot)
    keep = (jnp.arange(RMAX)[None, :] < rank[:, None]).astype(v_factor.dtype)
    masked = v_factor.reshape(NR, B, RMAX) * keep[:, None, :]
    rhs = masked.astype(jnp.float32).transpose(1, 0, 2).reshape(B, NR * RMAX)
    solved = lax.linalg.triangular_solve(lower, rhs, left_side=True, lower=True)
    gfac = solved.reshape(B, NR, RMAX).transpose(1, 0, 2).astype(jnp.bfloat16)
    ublk = u_factor.reshape(NR, B, RMAX)
    tcol = jnp.arange(wcols)
    cidx = (tcol // WC_DEV * per_dev + tcol % WC_DEV).astype(jnp.int32)
    update_term = schur_complement_term(ublk, gfac, ublk[cidx], gfac[cidx])
    return summed - update_term
```

```python
import functools

import jax
import jax.numpy as jnp
from jax import lax
from jax.experimental import pallas as pl
from jax.experimental.pallas import tpu as pltpu
from jax.sharding import PartitionSpec as P

MESH = pl.DeviceIdType.MESH
F32 = jnp.float32
BF16 = jnp.bfloat16


def exact_dot(a, b, contract):
    return lax.dot_general(
        a, b, (contract, ((), ())), precision=lax.Precision.HIGHEST, preferred_element_type=F32
    )


def inverse_factor(work):
    size = work.shape[0]
    rows = lax.broadcasted_iota(jnp.int32, (size, size), 0)
    lanes = lax.broadcasted_iota(jnp.int32, (size, size), 1)
    one_lane = lax.broadcasted_iota(jnp.int32, (1, size), 1)

    def step(k, carry):
        m = work[...]
        top = work[pl.ds(k, 1), :]
        pivot = jnp.sum(jnp.where(one_lane == k, top, 0.0), axis=1, keepdims=True)
        root = lax.rsqrt(pivot)
        root = root * (1.5 - 0.5 * pivot * root * root)
        column = jnp.sum(jnp.where(lanes == k, m, 0.0), axis=1, keepdims=True)
        scaled = jnp.where(one_lane == k, 1.0, top) * root
        factor = column * root
        below = jnp.where(lanes == k, 0.0, m) - factor * scaled
        work[...] = jnp.where(rows > k, below, jnp.where(rows == k, scaled, m))
        return carry

    lax.fori_loop(0, size, step, 0)
    work[...] = jnp.where(lanes <= rows, work[...], 0.0)


def split3(x):
    hi = x.astype(BF16)
    rest = x - hi.astype(F32)
    mid = rest.astype(BF16)
    low = (rest - mid.astype(F32)).astype(BF16)
    return hi, mid, low


def solve(parts, rhs):
    hi, mid, low = (jnp.dot(p, rhs, preferred_element_type=F32) for p in parts)
    return (hi + (mid + low)).astype(BF16)


def exchange_kernel(
    nr, nc, cap, per_dev,
    src_ref, labels_ref, contrib_ref, pivot_ref, vwide_ref, vfirst_ref, upack_ref,
    arr_ref, lab_ref, uall_ref, uc_ref, mid_ref,
    pack, piv, vc, mids, work1, work2,
    blk_s, blk_r, lab_s, lab_r, piv_s, piv_r, vc_s, vc_r, uc_s, uc_r, u_s, u_r, mid_s, mid_r, loc,
):
    n = nr * nc
    r = lax.axis_index("row")
    c = lax.axis_index("col")
    me = r * nc + c
    prows = pivot_ref.shape[0]
    half = vfirst_ref.shape[0]
    block = 2 * half
    rmax = vfirst_ref.shape[1] // 2

    def peer(s):
        return lax.rem(r + s // nc, nr), lax.rem(c + s % nc, nc)

    def flip(m):
        return c + m - 2 * m * lax.rem(c // m, 2)

    def remote(src, dst, ssem, rsem, rr, cc):
        return pltpu.make_async_remote_copy(
            src_ref=src, dst_ref=dst, send_sem=ssem, recv_sem=rsem,
            device_id={"row": rr, "col": cc}, device_id_type=MESH,
        )

    barrier = pltpu.get_barrier_semaphore()
    for s in range(1, n):
        rr, cc = peer(s)
        pl.semaphore_signal(barrier, inc=1, device_id={"row": rr, "col": cc}, device_id_type=MESH)
    pl.semaphore_wait(barrier, n - 1)

    order = sorted(range(1, n), key=lambda s: (min(s % nc, nc - s % nc) * -1, s // nc))

    pivot_copies, first_copies = [], []
    my_piv = piv.at[pl.ds(pl.multiple_of(me * prows, prows), prows)]
    for s in order:
        rr, cc = peer(s)
        copy = remote(pivot_ref, my_piv, piv_s.at[s], piv_r.at[s], rr, cc)
        copy.start()
        pivot_copies.append(copy)
    for s in order:
        rr, cc = peer(s)
        copy = remote(vfirst_ref, vc.at[c], vc_s.at[s], vc_r.at[s], rr, cc)
        pl.when(r == 0)(copy.start)
        first_copies.append((s, copy))
    column_copies = []
    for s in range(nc, n, nc):
        rr, cc = peer(s)
        copy = remote(upack_ref.at[pl.ds(0, half)], uc_ref, uc_s.at[s], uc_r.at[s], rr, cc)
        pl.when(r == 0)(copy.start)
        column_copies.append((s, copy))

    locals_ = [
        pltpu.make_async_copy(pivot_ref, my_piv, loc.at[0]),
        pltpu.make_async_copy(upack_ref, uall_ref.at[c], loc.at[1]),
        pltpu.make_async_copy(labels_ref.at[me], lab_ref.at[me], loc.at[2]),
    ]
    for copy in locals_:
        copy.start()
    own_v = pltpu.make_async_copy(vfirst_ref, vc.at[c], loc.at[3])
    own_u = pltpu.make_async_copy(upack_ref.at[pl.ds(0, half)], uc_ref, loc.at[4])

    @pl.when(r == 0)
    def _():
        own_v.start()
        own_u.start()

    masks = []
    m = nc // 2
    while m:
        masks.append(m)
        m //= 2
    u_copies, stage, sem = [], [], 0
    held = [[]]
    for m in masks:
        stage.append([(m, path, sem + q) for q, path in enumerate(held)])
        sem += len(held)
        held = held + [path + [m] for path in held]

    def start_stage(entries):
        for m, path, q in entries:
            origin = c
            for step in path:
                origin = origin + step - 2 * step * lax.rem(c // step, 2)
            source = upack_ref if not path else uall_ref.at[origin]
            copy = remote(source, uall_ref.at[origin], u_s.at[q], u_r.at[q], r, flip(m))
            copy.start()
            u_copies.append(copy)

    start_stage(stage[0])

    block_copies = []
    for s in order + [0]:
        rr, cc = peer(s)
        target = rr * nc + cc
        for k in range(cap):
            pack[s * cap + k] = contrib_ref[src_ref[target * cap + k]]
        mine = arr_ref.at[pl.ds(me * cap, cap)]
        packed = pack.at[pl.ds(s * cap, cap)]
        if s:
            copy = remote(packed, mine, blk_s.at[s], blk_r.at[s], rr, cc)
            copy.start()
            block_copies.append(copy)
            copy = remote(labels_ref.at[target], lab_ref.at[me], lab_s.at[s], lab_r.at[s], rr, cc)
            copy.start()
            block_copies.append(copy)
        else:
            copy = pltpu.make_async_copy(packed, mine, loc.at[5])
            copy.start()
            locals_.append(copy)

    locals_[0].wait()
    for copy in pivot_copies:
        copy.wait()

    work1[...] = piv[0:half, 0:half]
    inverse_factor(work1)
    inv1 = work1[...]
    low = exact_dot(piv[half:, 0:half], inv1, ((1,), (1,)))
    work2[...] = piv[half:, half:] - exact_dot(low, low, ((1,), (1,)))

    sent = 0
    for entries in stage[1:]:
        for copy in u_copies[sent:]:
            copy.wait_recv()
        sent = len(u_copies)
        start_stage(entries)

    inverse_factor(work2)
    inv2 = work2[...]
    inv21 = -exact_dot(inv2, exact_dot(low, inv1, ((1,), (0,))), ((1,), (0,)))
    inverse = jnp.concatenate(
        [
            jnp.concatenate([inv1, jnp.zeros_like(inv1)], axis=1),
            jnp.concatenate([inv21, inv2], axis=1),
        ],
        axis=0,
    )
    parts = split3(inverse)
    g_own = solve(parts, vwide_ref[...])

    @pl.when(r == 0)
    def _():
        own_v.wait()
        own_u.wait()

    for s, copy in first_copies:
        pl.when(r == 0)(copy.wait_send)
        pl.when(lax.rem(r + nr - s // nc, nr) == 0)(copy.wait_recv)

    mid_copies = []
    for t in range(nc):
        packed_v = vc[t]
        v_t = jnp.concatenate([packed_v[:, :rmax], packed_v[:, rmax:]], axis=0)
        g_t = solve(parts, v_t)
        middle = lax.dot_general(
            g_own, g_t, (((0,), (0,)), ((), ())), preferred_element_type=F32
        ).astype(BF16)
        for j in range((per_dev + 1) // 2):
            first = middle[2 * j * rmax : (2 * j + 1) * rmax]
            if 2 * j + 1 < per_dev:
                second = middle[(2 * j + 1) * rmax : (2 * j + 2) * rmax]
            else:
                second = jnp.zeros_like(first)
            mids[t, j * rmax : (j + 1) * rmax] = jnp.concatenate([first, second], axis=1)
    for s in range(1, nc):
        cc = lax.rem(c + s, nc)
        copy = remote(mids.at[cc], mid_ref.at[c], mid_s.at[s], mid_r.at[s], r, cc)
        copy.start()
        mid_copies.append(copy)
    copy = pltpu.make_async_copy(mids.at[c], mid_ref.at[c], loc.at[6])
    copy.start()
    locals_.append(copy)

    for copy in locals_[1:]:
        copy.wait()
    for s, copy in column_copies:
        pl.when(r == 0)(copy.wait_send)
        pl.when(lax.rem(r + nr - s // nc, nr) == 0)(copy.wait_recv)
    for copy in u_copies[:sent]:
        copy.wait_send()
    for copy in u_copies[sent:]:
        copy.wait()
    for copy in mid_copies + block_copies:
        copy.wait()


def update_kernel(cap, per_dev, lab_ref, parent_ref, arr_ref, u_ref, mid_ref, uc_ref, out_ref, head, nxt):
    step = pl.program_id(0)
    slots = arr_ref.shape[0]
    block = arr_ref.shape[1]
    half = u_ref.shape[2]
    rmax = half // 2

    @pl.when(step == 0)
    def _():
        for i in range(head.shape[0]):
            head[i] = -1

        def link(j, carry):
            label = lab_ref[j // cap, 0, lax.rem(j, cap)]

            @pl.when(label >= 0)
            def _():
                nxt[j] = head[label]
                head[label] = j

            return carry

        lax.fori_loop(0, slots, link, 0)

    uc = uc_ref[...]
    top, bottom = uc[:, :rmax], uc[:, rmax:]
    right = jnp.concatenate([top, bottom], axis=0)
    zero = jnp.zeros_like(right)
    right_top = jnp.concatenate([right, zero], axis=1)
    right_bottom = jnp.concatenate([zero, right], axis=1)
    for i in range(per_dev):
        j = i // 2
        middle = mid_ref[0, j * rmax : (j + 1) * rmax, (i % 2) * rmax : (i % 2 + 1) * rmax]
        blank = jnp.zeros_like(middle)
        spread = jnp.concatenate(
            [jnp.concatenate([middle, blank], axis=1), jnp.concatenate([blank, middle], axis=1)], axis=0
        )
        left = jnp.dot(
            u_ref[0, i * half : (i + 1) * half], spread, preferred_element_type=F32
        ).astype(BF16)
        rows = pl.ds(i * block, half)
        later = pl.ds(i * block + half, half)
        out_ref[rows] = parent_ref[rows].astype(F32) - lax.dot_general(
            left, right_top, (((1,), (1,)), ((), ())), preferred_element_type=F32
        )
        out_ref[later] = parent_ref[later].astype(F32) - lax.dot_general(
            left, right_bottom, (((1,), (1,)), ((), ())), preferred_element_type=F32
        )

        def add(j):
            out_ref[pl.ds(i * block, block)] += arr_ref[j].astype(F32)
            return nxt[j]

        lax.while_loop(lambda j: j >= 0, add, head[step * per_dev + i])


def on_device(parent, contrib, owner, slot, pivot, u_factor, v_factor, rank):
    nr = lax.axis_size("row")
    nc = lax.axis_size("col")
    n = nr * nc
    held, block, _ = contrib.shape
    cap = max(2, (held + n - 1) // n)
    rmax = u_factor.shape[1]
    per_dev = rank.shape[0]
    half = block // 2
    pairs = (per_dev + 1) // 2
    local_count = parent.shape[0] // block

    target = owner[:, 0]
    index = jnp.arange(held)
    earlier = (target[None, :] == target[:, None]) & (index[None, :] < index[:, None])
    dest = target * cap + jnp.sum(earlier, axis=1)
    hit = dest[None, :] == jnp.arange(n * cap)[:, None]
    source = jnp.sum(jnp.where(hit, index[None, :], 0), axis=1).astype(jnp.int32)
    label = (jnp.sum(jnp.where(hit, slot[None, :] + 1, 0), axis=1) - 1).astype(jnp.int32)
    labels = jnp.pad(label.reshape(n, 1, cap), ((0, 0), (0, 0), (0, 128 - cap)))

    keep = jnp.arange(rmax)[None, :] < rank[:, None]
    masked = jnp.where(keep[:, None, :], v_factor.reshape(per_dev, block, rmax), 0)
    v_wide = masked.transpose(1, 0, 2).reshape(block, per_dev * rmax)
    v_first = masked[0].reshape(2, half, rmax).transpose(1, 0, 2).reshape(half, 2 * rmax)
    u_pack = (
        u_factor.reshape(per_dev, 2, half, rmax).transpose(0, 2, 1, 3).reshape(per_dev * half, 2 * rmax)
    )

    dma = pltpu.SemaphoreType.DMA
    vmem = pl.BlockSpec(memory_space=pltpu.VMEM)
    anywhere = pl.BlockSpec(memory_space=pl.ANY)
    arrived, in_labels, u_all, u_col, mids = pl.pallas_call(
        functools.partial(exchange_kernel, nr, nc, cap, per_dev),
        out_shape=(
            jax.ShapeDtypeStruct((n * cap, block, block), contrib.dtype),
            jax.ShapeDtypeStruct((n, 1, 128), jnp.int32),
            jax.ShapeDtypeStruct((nc, per_dev * half, 2 * rmax), BF16),
            jax.ShapeDtypeStruct((half, 2 * rmax), BF16),
            jax.ShapeDtypeStruct((nc, pairs * rmax, 2 * rmax), BF16),
        ),
        in_specs=[
            pl.BlockSpec(memory_space=pltpu.SMEM), anywhere, vmem, vmem, vmem, vmem, anywhere,
        ],
        out_specs=(anywhere,) * 5,
        scratch_shapes=[
            pltpu.VMEM((n * cap, block, block), contrib.dtype),
            pltpu.VMEM((block, block), F32),
            pltpu.VMEM((nc, half, 2 * rmax), BF16),
            pltpu.VMEM((nc, pairs * rmax, 2 * rmax), BF16),
            pltpu.VMEM((half, half), F32),
            pltpu.VMEM((half, half), F32),
        ]
        + [dma((n,))] * 10
        + [dma((nc,))] * 4
        + [dma((7,))],
        compiler_params=pltpu.CompilerParams(
            collective_id=0, has_side_effects=True, vmem_limit_bytes=32 << 20
        ),
    )(source, labels, contrib, pivot, v_wide, v_first, u_pack)

    span = per_dev * block
    return pl.pallas_call(
        functools.partial(update_kernel, cap, per_dev),
        grid=(local_count // per_dev,),
        out_shape=jax.ShapeDtypeStruct(parent.shape, F32),
        in_specs=[
            pl.BlockSpec(memory_space=pltpu.SMEM),
            pl.BlockSpec((span, block), lambda i: (i, 0)),
            pl.BlockSpec((n * cap, block, block), lambda i: (0, 0, 0)),
            pl.BlockSpec((1, per_dev * half, 2 * rmax), lambda i: (i, 0, 0)),
            pl.BlockSpec((1, pairs * rmax, 2 * rmax), lambda i: (i, 0, 0)),
            pl.BlockSpec((half, 2 * rmax), lambda i: (0, 0)),
        ],
        out_specs=pl.BlockSpec((span, block), lambda i: (i, 0)),
        scratch_shapes=[pltpu.SMEM((local_count,), jnp.int32), pltpu.SMEM((n * cap,), jnp.int32)],
        compiler_params=pltpu.CompilerParams(vmem_limit_bytes=40 << 20),
    )(in_labels, parent, arrived, u_all, mids, u_col)


def solution(mesh):
    in_specs = (
        P(("front", "row"), "col"),
        P(("front", "row", "col"), None, None),
        P(("front", "row", "col"), None),
        P(("front", "row", "col")),
        P(("front", "row", "col"), None),
        P(("front", "row", "col"), None),
        P(("front", "row", "col"), None),
        P(("front", "row", "col")),
    )
    return jax.shard_map(
        on_device, mesh=mesh, in_specs=in_specs, out_specs=P(("front", "row"), "col"), check_vma=False
    )
```

```python
import functools

import jax
import jax.numpy as jnp
from jax import lax
from jax.experimental import pallas as pl
from jax.experimental.pallas import tpu as pltpu
from jax.sharding import PartitionSpec as P

MESH = pl.DeviceIdType.MESH
F32 = jnp.float32
BF16 = jnp.bfloat16
EARLY = 9


def exact_dot(a, b, contract):
    return lax.dot_general(
        a, b, (contract, ((), ())), precision=lax.Precision.HIGHEST, preferred_element_type=F32
    )


def inverse_factor(work):
    size = work.shape[0]
    rows = lax.broadcasted_iota(jnp.int32, (size, size), 0)
    lanes = lax.broadcasted_iota(jnp.int32, (size, size), 1)
    one_lane = lax.broadcasted_iota(jnp.int32, (1, size), 1)

    def step(k, carry):
        m = work[...]
        top = work[pl.ds(k, 1), :]
        pivot = jnp.sum(jnp.where(one_lane == k, top, 0.0), axis=1, keepdims=True)
        root = lax.rsqrt(pivot)
        root = root * (1.5 - 0.5 * pivot * root * root)
        column = jnp.sum(jnp.where(lanes == k, m, 0.0), axis=1, keepdims=True)
        scaled = jnp.where(one_lane == k, 1.0, top) * root
        factor = column * root
        below = jnp.where(lanes == k, 0.0, m) - factor * scaled
        work[...] = jnp.where(rows > k, below, jnp.where(rows == k, scaled, m))
        return carry

    lax.fori_loop(0, size, step, 0)
    work[...] = jnp.where(lanes <= rows, work[...], 0.0)


def split3(x):
    hi = x.astype(BF16)
    rest = x - hi.astype(F32)
    mid = rest.astype(BF16)
    low = (rest - mid.astype(F32)).astype(BF16)
    return hi, mid, low


def solve(parts, rhs_t):
    hi, mid, low = (
        lax.dot_general(rhs_t, p, (((1,), (1,)), ((), ())), preferred_element_type=F32) for p in parts
    )
    return (hi + (mid + low)).astype(BF16)


def exchange_kernel(
    nr, nc, cap, per_dev,
    owner_ref, slot_ref, rank_ref, contrib_ref, pivot_ref, vt_ref, ut_ref, parent_ref,
    arr_ref, lab_ref, base_ref,
    cbuf, pack, piv, vown, vfirst, vc, ug, uc, mid_out, mid_in, labels, par, work1, work2,
    blk_s, blk_r, lab_s, lab_r, piv1_s, piv1_r, v1_s, v1_r, u_s, u_r, mid_s, mid_r,
    piv2_s, piv2_r, v2_s, v2_r, uc_s, uc_r, loc,
):
    n = nr * nc
    r = lax.axis_index("row")
    c = lax.axis_index("col")
    me = r * nc + c
    held, block, _ = contrib_ref.shape
    prows = pivot_ref.shape[0]
    rmax = vt_ref.shape[0]
    half = block // 2

    def peer(s):
        return lax.rem(r + s // nc, nr), lax.rem(c + s % nc, nc)

    def flip(m):
        return c + m - 2 * m * lax.rem(c // m, 2)

    def remote(src, dst, ssem, rsem, rr, cc):
        return pltpu.make_async_remote_copy(
            src_ref=src, dst_ref=dst, send_sem=ssem, recv_sem=rsem,
            device_id={"row": rr, "col": cc}, device_id_type=MESH,
        )

    my_piv = piv.at[pl.ds(pl.multiple_of(me * prows, prows), prows)]
    row_piv = piv.at[pl.ds(pl.multiple_of(r * nc * prows, nc * prows), nc * prows)]
    my_vc = vc.at[pl.ds(pl.multiple_of(c * rmax, rmax), rmax)]
    first_u = ut_ref.at[:, pl.ds(0, block)]
    load_v = pltpu.make_async_copy(vt_ref, vown, loc.at[0])
    load_piv = pltpu.make_async_copy(pivot_ref, my_piv, loc.at[1])
    load_contrib = pltpu.make_async_copy(contrib_ref, cbuf, loc.at[2])
    load_u = pltpu.make_async_copy(ut_ref, ug.at[c], loc.at[3])
    load_uc = pltpu.make_async_copy(first_u, uc, loc.at[4])
    load_parent = pltpu.make_async_copy(parent_ref, par, loc.at[5])
    for copy in (load_v, load_piv, load_contrib, load_u, load_parent):
        copy.start()
    pl.when(r == 0)(load_uc.start)

    barrier = pltpu.get_barrier_semaphore()
    for s in range(1, n):
        rr, cc = peer(s)
        pl.semaphore_signal(barrier, inc=1, device_id={"row": rr, "col": cc}, device_id_type=MESH)
    load_v.wait()
    vfirst[...] = jnp.where(
        lax.broadcasted_iota(jnp.int32, (rmax, block), 0) < rank_ref[0], vown[:, 0:block], 0
    ).astype(BF16)
    pl.semaphore_wait(barrier, n - 1)

    pivot_1, pivot_2, first_1, first_2, column_u = [], [], [], [], []
    for s in range(1, nc):
        cc = lax.rem(c + s, nc)
        copy = remote(pivot_ref, my_piv, piv1_s.at[s], piv1_r.at[s], r, cc)
        copy.start()
        pivot_1.append(copy)
    for s in range(1, nc):
        cc = lax.rem(c + s, nc)
        copy = remote(vfirst, my_vc, v1_s.at[s], v1_r.at[s], r, cc)
        pl.when(r == 0)(copy.start)
        first_1.append(copy)

    masks = []
    m = nc // 2
    while m:
        masks.append(m)
        m //= 2
    u_copies, stages, sem, paths = [], [], 0, [[]]
    for m in masks:
        stages.append([(m, path, sem + q) for q, path in enumerate(paths)])
        sem += len(paths)
        paths = paths + [path + [m] for path in paths]

    def start_stage(entries):
        for m, path, q in entries:
            origin = c
            for step in path:
                origin = origin + step - 2 * step * lax.rem(c // step, 2)
            source = ug.at[origin] if path else ut_ref
            copy = remote(source, ug.at[origin], u_s.at[q], u_r.at[q], r, flip(m))
            copy.start()
            u_copies.append(copy)

    start_stage(stages[0])

    lane = lax.broadcasted_iota(jnp.int32, (1, 128), 1)

    def pack_for(s):
        rr, cc = peer(s)
        target = rr * nc + cc

        def look(j, carry):
            count, found = carry[0], carry[1:]
            hit = owner_ref[j] == target
            found = [jnp.where(hit & (count == k), j, found[k]) for k in range(cap)]
            return (jnp.where(hit, count + 1, count), *found)

        count, *found = lax.fori_loop(0, held, look, (jnp.int32(0),) * (cap + 1))
        row = jnp.full((1, 128), -1, jnp.int32)
        for k in range(cap):
            pack[s * cap + k] = cbuf[found[k]]
            row = jnp.where(lane == k, jnp.where(count > k, slot_ref[found[k]], -1), row)
        labels[s] = row

    mine = arr_ref.at[pl.ds(me * cap, cap)]
    block_copies = []

    def send(s):
        rr, cc = peer(s)
        copies = (
            remote(pack.at[pl.ds(s * cap, cap)], mine, blk_s.at[s], blk_r.at[s], rr, cc),
            remote(labels.at[s], lab_ref.at[me], lab_s.at[s], lab_r.at[s], rr, cc),
        )
        for copy in copies:
            copy.start()
            block_copies.append(copy)

    order = sorted(range(1, n), key=lambda s: (-min(s % nc, nc - s % nc), s // nc))
    early = order[: (EARLY * len(order)) // 16]
    late = order[len(early) :]
    ahead = early[: nc // 2]
    load_contrib.wait()
    for s in ahead:
        pack_for(s)

    load_piv.wait()
    for copy in pivot_1:
        copy.wait_recv()
    for s in range(1, nr):
        rr = lax.rem(r + s, nr)
        copy = remote(row_piv, row_piv, piv2_s.at[s], piv2_r.at[s], rr, c)
        copy.start()
        pivot_2.append(copy)

    @pl.when(r == 0)
    def _():
        vc[pl.ds(pl.multiple_of(c * rmax, rmax), rmax)] = vfirst[...]
        for copy in first_1:
            copy.wait_recv()

    for s in range(1, nr):
        rr = lax.rem(r + s, nr)
        copy = remote(vc, vc, v2_s.at[s], v2_r.at[s], rr, c)
        pl.when(r == 0)(copy.start)
        first_2.append((s, copy))
        copy = remote(first_u, uc, uc_s.at[s], uc_r.at[s], rr, c)
        pl.when(r == 0)(copy.start)
        column_u.append((s, copy))

    for s in ahead:
        send(s)
    for s in early[len(ahead) :]:
        pack_for(s)
        send(s)
    for s in late + [0]:
        pack_for(s)
    own = [
        pltpu.make_async_copy(pack.at[pl.ds(0, cap)], mine, loc.at[6]),
        pltpu.make_async_copy(labels.at[0], lab_ref.at[me], loc.at[7]),
    ]
    for copy in own:
        copy.start()

    for copy in pivot_2:
        copy.wait_recv()

    work1[...] = piv[0:half, 0:half]
    inverse_factor(work1)
    inv1 = work1[...]
    low = exact_dot(piv[half:, 0:half], inv1, ((1,), (1,)))
    work2[...] = piv[half:, half:] - exact_dot(low, low, ((1,), (1,)))

    sent = 0
    for entries in stages[1:]:
        for copy in u_copies[sent:]:
            copy.wait_recv()
        sent = len(u_copies)
        start_stage(entries)

    inverse_factor(work2)
    inv2 = work2[...]
    inv21 = -exact_dot(inv2, exact_dot(low, inv1, ((1,), (0,))), ((1,), (0,)))
    inverse = jnp.concatenate(
        [
            jnp.concatenate([inv1, jnp.zeros_like(inv1)], axis=1),
            jnp.concatenate([inv21, inv2], axis=1),
        ],
        axis=0,
    )
    parts = split3(inverse)
    place = lax.broadcasted_iota(jnp.int32, (rmax, block), 0)
    masked = [
        jnp.where(place < rank_ref[i], vown[:, i * block : (i + 1) * block], 0).astype(BF16)
        for i in range(per_dev)
    ]
    g_own = solve(parts, jnp.concatenate(masked, axis=0))

    for s, copy in first_2:
        pl.when(r == 0)(copy.wait_send)
        pl.when(lax.rem(r + nr - s, nr) == 0)(copy.wait_recv)
    g_columns = solve(parts, vc[...])
    mid_out[...] = lax.dot_general(
        g_columns, g_own, (((1,), (1,)), ((), ())), preferred_element_type=F32
    ).astype(BF16)
    mid_copies = []
    for s in range(1, nc):
        cc = lax.rem(c + s, nc)
        rows = mid_out.at[pl.ds(pl.multiple_of(cc * rmax, rmax), rmax)]
        copy = remote(rows, mid_in.at[c], mid_s.at[s], mid_r.at[s], r, cc)
        copy.start()
        mid_copies.append(copy)
    for s in late:
        send(s)
    mid_in[c] = mid_out[pl.ds(pl.multiple_of(c * rmax, rmax), rmax)]

    load_u.wait()
    load_parent.wait()
    pl.when(r == 0)(load_uc.wait)
    for s, copy in column_u:
        pl.when(r == 0)(copy.wait_send)
        pl.when(lax.rem(r + nr - s, nr) == 0)(copy.wait_recv)
    for copy in u_copies[:sent]:
        copy.wait_send()
    for copy in u_copies[sent:]:
        copy.wait()
    for copy in mid_copies:
        copy.wait()

    right = uc[...]

    def update(q, carry):
        for i in range(per_dev):
            left = jnp.dot(
                mid_in[q, :, i * rmax : (i + 1) * rmax],
                ug[q, :, i * block : (i + 1) * block],
                preferred_element_type=F32,
            ).astype(BF16)
            rows = pl.ds(pl.multiple_of((q * per_dev + i) * block, block), block)
            base_ref[rows] = par[rows].astype(F32) - lax.dot_general(
                left, right, (((0,), (0,)), ((), ())), preferred_element_type=F32
            )
        return carry

    lax.fori_loop(0, nc, update, 0)

    for copy in pivot_1 + pivot_2:
        copy.wait_send()

    @pl.when(r == 0)
    def _():
        for copy in first_1:
            copy.wait_send()

    for copy in own:
        copy.wait()
    for copy in block_copies:
        copy.wait()


def add_kernel(cap, lab_ref, base_ref, arr_ref, out_ref, total, head, nxt, done):
    slots, block, _ = arr_ref.shape
    places = head.shape[0]

    def clear(i, carry):
        head[i] = -1
        return carry

    def link(j, carry):
        label = lab_ref[j // cap, 0, lax.rem(j, cap)]

        @pl.when(label >= 0)
        def _():
            nxt[j] = head[label]
            head[label] = j

        return carry

    lax.fori_loop(0, places, clear, 0)
    lax.fori_loop(0, slots, link, 0)

    def each(i, carry):
        rows = pl.ds(pl.multiple_of(i * block, block), block)
        first = head[i]

        @pl.when(first < 0)
        def _():
            pltpu.make_async_copy(base_ref.at[rows], out_ref.at[rows], done.at[i]).start()

        @pl.when(first >= 0)
        def _():
            total[rows] = base_ref[rows] + arr_ref[first].astype(F32)

            def add(j):
                total[rows] += arr_ref[j].astype(F32)
                return nxt[j]

            lax.while_loop(lambda j: j >= 0, add, nxt[first])
            pltpu.make_async_copy(total.at[rows], out_ref.at[rows], done.at[i]).start()

        return carry

    lax.fori_loop(0, places, each, 0)

    def finish(i, carry):
        rows = pl.ds(pl.multiple_of(i * block, block), block)
        pltpu.make_async_copy(total.at[rows], out_ref.at[rows], done.at[i]).wait()
        return carry

    lax.fori_loop(0, places, finish, 0)


def on_device(parent, contrib, owner, slot, pivot, u_factor, v_factor, rank):
    nr = lax.axis_size("row")
    nc = lax.axis_size("col")
    n = nr * nc
    held, block, _ = contrib.shape
    cap = max(2, (held + n - 1) // n)
    rmax = u_factor.shape[1]
    per_dev = rank.shape[0]
    half = block // 2
    slots = n * cap

    dma = pltpu.SemaphoreType.DMA
    vmem = pl.BlockSpec(memory_space=pltpu.VMEM)
    smem = pl.BlockSpec(memory_space=pltpu.SMEM)
    anywhere = pl.BlockSpec(memory_space=pl.ANY)
    arrived, in_labels, base = pl.pallas_call(
        functools.partial(exchange_kernel, nr, nc, cap, per_dev),
        out_shape=(
            jax.ShapeDtypeStruct((slots, block, block), contrib.dtype),
            jax.ShapeDtypeStruct((n, 1, 128), jnp.int32),
            jax.ShapeDtypeStruct(parent.shape, F32),
        ),
        in_specs=[smem] * 3 + [pl.BlockSpec(memory_space=pltpu.HBM)] * 5,
        out_specs=(anywhere, anywhere, vmem),
        scratch_shapes=[
            pltpu.VMEM(contrib.shape, contrib.dtype),
            pltpu.VMEM((slots, block, block), contrib.dtype),
            pltpu.VMEM((block, block), F32),
            pltpu.VMEM((rmax, per_dev * block), BF16),
            pltpu.VMEM((rmax, block), BF16),
            pltpu.VMEM((nc * rmax, block), BF16),
            pltpu.VMEM((nc, rmax, per_dev * block), BF16),
            pltpu.VMEM((rmax, block), BF16),
            pltpu.VMEM((nc * rmax, per_dev * rmax), BF16),
            pltpu.VMEM((nc, rmax, per_dev * rmax), BF16),
            pltpu.VMEM((n, 1, 128), jnp.int32),
            pltpu.VMEM(parent.shape, parent.dtype),
            pltpu.VMEM((half, half), F32),
            pltpu.VMEM((half, half), F32),
        ]
        + [dma((n,))] * 4
        + [dma((nc,))] * 8
        + [dma((nr,))] * 6
        + [dma((8,))],
        compiler_params=pltpu.CompilerParams(
            collective_id=0, has_side_effects=True, vmem_limit_bytes=28 << 20
        ),
    )(owner[:, 0], slot, rank, contrib, pivot, v_factor.T, u_factor.T, parent)

    places = parent.shape[0] // block
    return pl.pallas_call(
        functools.partial(add_kernel, cap),
        out_shape=jax.ShapeDtypeStruct(parent.shape, F32),
        in_specs=[smem, vmem, vmem],
        out_specs=anywhere,
        scratch_shapes=[
            pltpu.VMEM(parent.shape, F32),
            pltpu.SMEM((places,), jnp.int32),
            pltpu.SMEM((slots,), jnp.int32),
            dma((places,)),
        ],
        compiler_params=pltpu.CompilerParams(vmem_limit_bytes=24 << 20),
    )(in_labels, base, arrived)


def solution(mesh):
    in_specs = (
        P(("front", "row"), "col"),
        P(("front", "row", "col"), None, None),
        P(("front", "row", "col"), None),
        P(("front", "row", "col")),
        P(("front", "row", "col"), None),
        P(("front", "row", "col"), None),
        P(("front", "row", "col"), None),
        P(("front", "row", "col")),
    )
    return jax.shard_map(
        on_device, mesh=mesh, in_specs=in_specs, out_specs=P(("front", "row"), "col"), check_vma=False
    )
```

```python
import functools

import jax
import jax.numpy as jnp
from jax import lax
from jax.experimental import pallas as pl
from jax.experimental.pallas import tpu as pltpu
from jax.sharding import PartitionSpec as P

MESH = pl.DeviceIdType.MESH
F32 = jnp.float32
BF16 = jnp.bfloat16
EARLY = 9


def exact_dot(a, b, contract):
    return lax.dot_general(
        a, b, (contract, ((), ())), precision=lax.Precision.HIGHEST, preferred_element_type=F32
    )


def inverse_factor(work):
    size = work.shape[0]
    rows = lax.broadcasted_iota(jnp.int32, (size, size), 0)
    lanes = lax.broadcasted_iota(jnp.int32, (size, size), 1)
    one_lane = lax.broadcasted_iota(jnp.int32, (1, size), 1)

    def step(k, carry):
        m = work[...]
        top = work[pl.ds(k, 1), :]
        pivot = jnp.sum(jnp.where(one_lane == k, top, 0.0), axis=1, keepdims=True)
        root = lax.rsqrt(pivot)
        root = root * (1.5 - 0.5 * pivot * root * root)
        column = jnp.sum(jnp.where(lanes == k, m, 0.0), axis=1, keepdims=True)
        scaled = jnp.where(one_lane == k, 1.0, top) * root
        factor = column * root
        below = jnp.where(lanes == k, 0.0, m) - factor * scaled
        work[...] = jnp.where(rows > k, below, jnp.where(rows == k, scaled, m))
        return carry

    lax.fori_loop(0, size, step, 0)
    work[...] = jnp.where(lanes <= rows, work[...], 0.0)


def split3(x):
    hi = x.astype(BF16)
    rest = x - hi.astype(F32)
    mid = rest.astype(BF16)
    low = (rest - mid.astype(F32)).astype(BF16)
    return hi, mid, low


def solve(parts, rhs_t):
    hi, mid, low = (
        lax.dot_general(rhs_t, p, (((1,), (1,)), ((), ())), preferred_element_type=F32) for p in parts
    )
    return (hi + (mid + low)).astype(BF16)


def exchange_kernel(
    nr, nc, cap, per_dev,
    ints_ref, contrib_ref, pivot_ref, vt_ref, ut_ref,
    arr_ref, lab_ref, term_ref,
    cbuf, pack, piv, vown, vfirst, vc, ug, uc, mid_out, mid_in, labels, work1, work2,
    blk_s, blk_r, lab_s, lab_r, piv1_s, piv1_r, v1_s, v1_r, u_s, u_r, mid_s, mid_r,
    piv2_s, piv2_r, v2_s, v2_r, uc_s, uc_r, loc,
):
    n = nr * nc
    r = lax.axis_index("row")
    c = lax.axis_index("col")
    me = r * nc + c
    held, block, _ = contrib_ref.shape
    prows = pivot_ref.shape[0]
    rmax = vt_ref.shape[0]
    half = block // 2

    wing = nc // 2

    def peer(s):
        side = lax.rem(c // wing + (s % nc) // wing, 2)
        return lax.rem(r + s // nc, nr), side * wing + lax.rem(lax.rem(c, wing) + s % wing, wing)

    def flip(m):
        return c + m - 2 * m * lax.rem(c // m, 2)

    def remote(src, dst, ssem, rsem, rr, cc):
        return pltpu.make_async_remote_copy(
            src_ref=src, dst_ref=dst, send_sem=ssem, recv_sem=rsem,
            device_id={"row": rr, "col": cc}, device_id_type=MESH,
        )

    my_piv = piv.at[pl.ds(pl.multiple_of(me * prows, prows), prows)]
    row_piv = piv.at[pl.ds(pl.multiple_of(r * nc * prows, nc * prows), nc * prows)]
    my_vc = vc.at[pl.ds(pl.multiple_of(c * rmax, rmax), rmax)]
    first_u = ut_ref.at[:, pl.ds(0, block)]
    load_v = pltpu.make_async_copy(vt_ref, vown, loc.at[0])
    load_piv = pltpu.make_async_copy(pivot_ref, my_piv, loc.at[1])
    load_contrib = pltpu.make_async_copy(contrib_ref, cbuf, loc.at[2])
    load_u = pltpu.make_async_copy(ut_ref, ug.at[c], loc.at[3])
    load_uc = pltpu.make_async_copy(first_u, uc, loc.at[4])
    for copy in (load_v, load_piv, load_contrib, load_u):
        copy.start()
    pl.when(r == 0)(load_uc.start)

    barrier = pltpu.get_barrier_semaphore()
    for s in range(1, n):
        rr, cc = peer(s)
        pl.semaphore_signal(barrier, inc=1, device_id={"row": rr, "col": cc}, device_id_type=MESH)
    load_v.wait()
    vfirst[...] = jnp.where(
        lax.broadcasted_iota(jnp.int32, (rmax, block), 0) < ints_ref[2 * held], vown[:, 0:block], 0
    ).astype(BF16)
    pl.semaphore_wait(barrier, n - 1)

    pivot_1, pivot_2, first_1, first_2, column_u = [], [], [], [], []
    for s in range(1, nc):
        cc = lax.rem(c + s, nc)
        copy = remote(pivot_ref, my_piv, piv1_s.at[s], piv1_r.at[s], r, cc)
        copy.start()
        pivot_1.append(copy)
    for s in range(1, nc):
        cc = lax.rem(c + s, nc)
        copy = remote(vfirst, my_vc, v1_s.at[s], v1_r.at[s], r, cc)
        pl.when(r == 0)(copy.start)
        first_1.append(copy)

    masks = []
    m = nc // 2
    while m:
        masks.append(m)
        m //= 2
    u_copies, stages, sem, paths = [], [], 0, [[]]
    for m in masks:
        stages.append([(m, path, sem + q) for q, path in enumerate(paths)])
        sem += len(paths)
        paths = paths + [path + [m] for path in paths]

    def start_stage(entries):
        for m, path, q in entries:
            origin = c
            for step in path:
                origin = origin + step - 2 * step * lax.rem(c // step, 2)
            source = ug.at[origin] if path else ut_ref
            copy = remote(source, ug.at[origin], u_s.at[q], u_r.at[q], r, flip(m))
            copy.start()
            u_copies.append(copy)

    start_stage(stages[0])

    lane = lax.broadcasted_iota(jnp.int32, (1, 128), 1)

    def pack_for(s):
        rr, cc = peer(s)
        target = rr * nc + cc

        def look(j, carry):
            count, found = carry[0], carry[1:]
            hit = ints_ref[j] == target
            found = [jnp.where(hit & (count == k), j, found[k]) for k in range(cap)]
            return (jnp.where(hit, count + 1, count), *found)

        count, *found = lax.fori_loop(0, held, look, (jnp.int32(0),) * (cap + 1))
        row = jnp.full((1, 128), -1, jnp.int32)
        for k in range(cap):
            pack[s * cap + k] = cbuf[found[k]]
            row = jnp.where(lane == k, jnp.where(count > k, ints_ref[held + found[k]], -1), row)
        labels[s] = row

    mine = arr_ref.at[pl.ds(me * cap, cap)]
    block_copies = []

    def send(s):
        rr, cc = peer(s)
        copies = (
            remote(pack.at[pl.ds(s * cap, cap)], mine, blk_s.at[s], blk_r.at[s], rr, cc),
            remote(labels.at[s], lab_ref.at[me], lab_s.at[s], lab_r.at[s], rr, cc),
        )
        for copy in copies:
            copy.start()
            block_copies.append(copy)

    far = [s for s in range(1, n) if s % nc >= wing]
    near = [s for s in range(1, n) if s % nc < wing]
    order = [s for pair in zip(far, near + [0]) for s in pair if s]
    early = order[: (EARLY * len(order)) // 16]
    late = order[len(early) :]
    ahead = early[: nc // 2]
    load_contrib.wait()
    for s in ahead:
        pack_for(s)

    load_piv.wait()
    for copy in pivot_1:
        copy.wait_recv()
    for s in range(1, nr):
        rr = lax.rem(r + s, nr)
        copy = remote(row_piv, row_piv, piv2_s.at[s], piv2_r.at[s], rr, c)
        copy.start()
        pivot_2.append(copy)

    @pl.when(r == 0)
    def _():
        vc[pl.ds(pl.multiple_of(c * rmax, rmax), rmax)] = vfirst[...]
        for copy in first_1:
            copy.wait_recv()

    for s in range(1, nr):
        rr = lax.rem(r + s, nr)
        copy = remote(vc, vc, v2_s.at[s], v2_r.at[s], rr, c)
        pl.when(r == 0)(copy.start)
        first_2.append((s, copy))
        copy = remote(first_u, uc, uc_s.at[s], uc_r.at[s], rr, c)
        pl.when(r == 0)(copy.start)
        column_u.append((s, copy))

    for s in ahead:
        send(s)
    for s in early[len(ahead) :]:
        pack_for(s)
        send(s)
    for s in late + [0]:
        pack_for(s)
    own = [
        pltpu.make_async_copy(pack.at[pl.ds(0, cap)], mine, loc.at[6]),
        pltpu.make_async_copy(labels.at[0], lab_ref.at[me], loc.at[7]),
    ]
    for copy in own:
        copy.start()

    for copy in pivot_2:
        copy.wait_recv()

    work1[...] = piv[0:half, 0:half]
    inverse_factor(work1)
    inv1 = work1[...]
    low = exact_dot(piv[half:, 0:half], inv1, ((1,), (1,)))
    work2[...] = piv[half:, half:] - exact_dot(low, low, ((1,), (1,)))

    sent = 0
    for entries in stages[1:]:
        for copy in u_copies[sent:]:
            copy.wait_recv()
        sent = len(u_copies)
        start_stage(entries)

    inverse_factor(work2)
    inv2 = work2[...]
    inv21 = -exact_dot(inv2, exact_dot(low, inv1, ((1,), (0,))), ((1,), (0,)))
    inverse = jnp.concatenate(
        [
            jnp.concatenate([inv1, jnp.zeros_like(inv1)], axis=1),
            jnp.concatenate([inv21, inv2], axis=1),
        ],
        axis=0,
    )
    parts = split3(inverse)
    place = lax.broadcasted_iota(jnp.int32, (rmax, block), 0)
    masked = [
        jnp.where(place < ints_ref[2 * held + i], vown[:, i * block : (i + 1) * block], 0).astype(BF16)
        for i in range(per_dev)
    ]
    g_own = solve(parts, jnp.concatenate(masked, axis=0))

    for s, copy in first_2:
        pl.when(r == 0)(copy.wait_send)
        pl.when(lax.rem(r + nr - s, nr) == 0)(copy.wait_recv)
    g_columns = solve(parts, vc[...])
    mid_out[...] = lax.dot_general(
        g_columns, g_own, (((1,), (1,)), ((), ())), preferred_element_type=F32
    ).astype(BF16)
    mid_copies = []
    for s in range(1, nc):
        cc = lax.rem(c + s, nc)
        rows = mid_out.at[pl.ds(pl.multiple_of(cc * rmax, rmax), rmax)]
        copy = remote(rows, mid_in.at[c], mid_s.at[s], mid_r.at[s], r, cc)
        copy.start()
        mid_copies.append(copy)
    for s in late:
        send(s)
    mid_in[c] = mid_out[pl.ds(pl.multiple_of(c * rmax, rmax), rmax)]

    load_u.wait()
    pl.when(r == 0)(load_uc.wait)
    for s, copy in column_u:
        pl.when(r == 0)(copy.wait_send)
        pl.when(lax.rem(r + nr - s, nr) == 0)(copy.wait_recv)
    for copy in u_copies[:sent]:
        copy.wait_send()
    for copy in u_copies[sent:]:
        copy.wait()
    for copy in mid_copies:
        copy.wait()

    right = uc[...]

    def update(q, carry):
        for i in range(per_dev):
            left = jnp.dot(
                mid_in[q, :, i * rmax : (i + 1) * rmax],
                ug[q, :, i * block : (i + 1) * block],
                preferred_element_type=F32,
            ).astype(BF16)
            rows = pl.ds(pl.multiple_of((q * per_dev + i) * block, block), block)
            term_ref[rows] = lax.dot_general(
                left, right, (((0,), (0,)), ((), ())), preferred_element_type=F32
            )
        return carry

    lax.fori_loop(0, nc, update, 0)

    for copy in pivot_1 + pivot_2:
        copy.wait_send()

    @pl.when(r == 0)
    def _():
        for copy in first_1:
            copy.wait_send()

    for copy in own:
        copy.wait()
    for copy in block_copies:
        copy.wait()


def add_kernel(cap, lab_ref, parent_ref, term_ref, arr_ref, out_ref, total, head, nxt, done):
    slots, block, _ = arr_ref.shape
    places = head.shape[0]

    def clear(i, carry):
        head[i] = -1
        return carry

    def link(j, carry):
        label = lab_ref[j // cap, 0, lax.rem(j, cap)]

        @pl.when(label >= 0)
        def _():
            nxt[j] = head[label]
            head[label] = j

        return carry

    lax.fori_loop(0, places, clear, 0)
    lax.fori_loop(0, slots, link, 0)

    def each(i, carry):
        rows = pl.ds(pl.multiple_of(i * block, block), block)
        first = head[i]

        @pl.when(first < 0)
        def _():
            total[rows] = parent_ref[rows].astype(F32) - term_ref[rows]

        @pl.when(first >= 0)
        def _():
            total[rows] = parent_ref[rows].astype(F32) + arr_ref[first].astype(F32) - term_ref[rows]

            def add(j):
                total[rows] += arr_ref[j].astype(F32)
                return nxt[j]

            lax.while_loop(lambda j: j >= 0, add, nxt[first])

        pltpu.make_async_copy(total.at[rows], out_ref.at[rows], done.at[i]).start()

        return carry

    lax.fori_loop(0, places, each, 0)

    def finish(i, carry):
        rows = pl.ds(pl.multiple_of(i * block, block), block)
        pltpu.make_async_copy(total.at[rows], out_ref.at[rows], done.at[i]).wait()
        return carry

    lax.fori_loop(0, places, finish, 0)


def on_device(parent, contrib, owner, slot, pivot, u_factor, v_factor, rank):
    nr = lax.axis_size("row")
    nc = lax.axis_size("col")
    n = nr * nc
    held, block, _ = contrib.shape
    cap = max(2, (held + n - 1) // n)
    rmax = u_factor.shape[1]
    per_dev = rank.shape[0]
    half = block // 2
    slots = n * cap

    dma = pltpu.SemaphoreType.DMA
    vmem = pl.BlockSpec(memory_space=pltpu.VMEM)
    smem = pl.BlockSpec(memory_space=pltpu.SMEM)
    anywhere = pl.BlockSpec(memory_space=pl.ANY)
    arrived, in_labels, term = pl.pallas_call(
        functools.partial(exchange_kernel, nr, nc, cap, per_dev),
        out_shape=(
            jax.ShapeDtypeStruct((slots, block, block), contrib.dtype),
            jax.ShapeDtypeStruct((n, 1, 128), jnp.int32),
            jax.ShapeDtypeStruct(parent.shape, F32),
        ),
        in_specs=[smem] + [anywhere] * 4,
        out_specs=(anywhere, anywhere, vmem),
        scratch_shapes=[
            pltpu.VMEM(contrib.shape, contrib.dtype),
            pltpu.VMEM((slots, block, block), contrib.dtype),
            pltpu.VMEM((block, block), F32),
            pltpu.VMEM((rmax, per_dev * block), BF16),
            pltpu.VMEM((rmax, block), BF16),
            pltpu.VMEM((nc * rmax, block), BF16),
            pltpu.VMEM((nc, rmax, per_dev * block), BF16),
            pltpu.VMEM((rmax, block), BF16),
            pltpu.VMEM((nc * rmax, per_dev * rmax), BF16),
            pltpu.VMEM((nc, rmax, per_dev * rmax), BF16),
            pltpu.VMEM((n, 1, 128), jnp.int32),
            pltpu.VMEM((half, half), F32),
            pltpu.VMEM((half, half), F32),
        ]
        + [dma((n,))] * 4
        + [dma((nc,))] * 8
        + [dma((nr,))] * 6
        + [dma((8,))],
        compiler_params=pltpu.CompilerParams(
            collective_id=0, has_side_effects=True, vmem_limit_bytes=28 << 20
        ),
    )(jnp.concatenate([owner[:, 0], slot, rank]), contrib, pivot, v_factor.T, u_factor.T)

    places = parent.shape[0] // block
    return pl.pallas_call(
        functools.partial(add_kernel, cap),
        out_shape=jax.ShapeDtypeStruct(parent.shape, F32),
        in_specs=[smem, vmem, vmem, vmem],
        out_specs=anywhere,
        scratch_shapes=[
            pltpu.VMEM(parent.shape, F32),
            pltpu.SMEM((places,), jnp.int32),
            pltpu.SMEM((slots,), jnp.int32),
            dma((places,)),
        ],
        compiler_params=pltpu.CompilerParams(vmem_limit_bytes=24 << 20),
    )(in_labels, parent, term, arrived)


def solution(mesh):
    in_specs = (
        P(("front", "row"), "col"),
        P(("front", "row", "col"), None, None),
        P(("front", "row", "col"), None),
        P(("front", "row", "col")),
        P(("front", "row", "col"), None),
        P(("front", "row", "col"), None),
        P(("front", "row", "col"), None),
        P(("front", "row", "col")),
    )
    return jax.shard_map(
        on_device, mesh=mesh, in_specs=in_specs, out_specs=P(("front", "row"), "col"), check_vma=False
    )
```

```python
import functools

import jax
import jax.numpy as jnp
from jax import lax
from jax.experimental import pallas as pl
from jax.experimental.pallas import tpu as pltpu
from jax.sharding import PartitionSpec as P

MESH = pl.DeviceIdType.MESH
F32 = jnp.float32
BF16 = jnp.bfloat16
EARLY = 9


def exact_dot(a, b, contract):
    return lax.dot_general(
        a, b, (contract, ((), ())), precision=lax.Precision.HIGHEST, preferred_element_type=F32
    )


def inverse_factor(work):
    size = work.shape[0]
    rows = lax.broadcasted_iota(jnp.int32, (size, size), 0)
    lanes = lax.broadcasted_iota(jnp.int32, (size, size), 1)
    one_lane = lax.broadcasted_iota(jnp.int32, (1, size), 1)

    def step(k, carry):
        m = work[...]
        top = work[pl.ds(k, 1), :]
        pivot = jnp.sum(jnp.where(one_lane == k, top, 0.0), axis=1, keepdims=True)
        root = lax.rsqrt(pivot)
        root = root * (1.5 - 0.5 * pivot * root * root)
        column = jnp.sum(jnp.where(lanes == k, m, 0.0), axis=1, keepdims=True)
        scaled = jnp.where(one_lane == k, 1.0, top) * root
        factor = column * root
        below = jnp.where(lanes == k, 0.0, m) - factor * scaled
        work[...] = jnp.where(rows > k, below, jnp.where(rows == k, scaled, m))
        return carry

    lax.fori_loop(0, size, step, 0)
    work[...] = jnp.where(lanes <= rows, work[...], 0.0)


def split3(x):
    hi = x.astype(BF16)
    rest = x - hi.astype(F32)
    mid = rest.astype(BF16)
    low = (rest - mid.astype(F32)).astype(BF16)
    return hi, mid, low


def solve(parts, rhs_t):
    hi, mid, low = (
        lax.dot_general(rhs_t, p, (((1,), (1,)), ((), ())), preferred_element_type=F32) for p in parts
    )
    return (hi + (mid + low)).astype(BF16)


def exchange_kernel(
    nr, nc, cap, per_dev,
    ints_ref, contrib_ref, pivot_ref, both_ref,
    arr_ref, lab_ref, term_ref,
    pack, piv, vfirst, vc, ug, uc, mid_out, mid_in, labels, work1, work2,
    blk_s, blk_r, lab_s, lab_r, piv1_s, piv1_r, v1_s, v1_r, u_s, u_r, mid_s, mid_r,
    piv2_s, piv2_r, v2_s, v2_r, uc_s, uc_r, loc,
):
    n = nr * nc
    r = lax.axis_index("row")
    c = lax.axis_index("col")
    me = r * nc + c
    held, block, _ = contrib_ref.shape
    prows = pivot_ref.shape[0]
    rmax = both_ref.shape[0] // 2
    vt_ref = both_ref.at[pl.ds(0, rmax)]
    ut_ref = both_ref.at[pl.ds(rmax, rmax)]
    half = block // 2

    wing = nc // 2

    def peer(s):
        side = lax.rem(c // wing + (s % nc) // wing, 2)
        return lax.rem(r + s // nc, nr), side * wing + lax.rem(lax.rem(c, wing) + s % wing, wing)

    def flip(m):
        return c + m - 2 * m * lax.rem(c // m, 2)

    def remote(src, dst, ssem, rsem, rr, cc):
        return pltpu.make_async_remote_copy(
            src_ref=src, dst_ref=dst, send_sem=ssem, recv_sem=rsem,
            device_id={"row": rr, "col": cc}, device_id_type=MESH,
        )

    my_piv = piv.at[pl.ds(pl.multiple_of(me * prows, prows), prows)]
    row_piv = piv.at[pl.ds(pl.multiple_of(r * nc * prows, nc * prows), nc * prows)]
    my_vc = vc.at[pl.ds(pl.multiple_of(c * rmax, rmax), rmax)]
    first_u = both_ref.at[pl.ds(rmax, rmax), pl.ds(0, block)]
    load_u = pltpu.make_async_copy(ut_ref, ug.at[c], loc.at[0])
    load_uc = pltpu.make_async_copy(first_u, uc, loc.at[1])
    barrier = pltpu.get_barrier_semaphore()
    for s in range(1, n):
        rr, cc = peer(s)
        pl.semaphore_signal(barrier, inc=1, device_id={"row": rr, "col": cc}, device_id_type=MESH)
    load_u.start()
    pl.when(r == 0)(load_uc.start)
    piv[pl.ds(pl.multiple_of(me * prows, prows), prows)] = pivot_ref[...]
    vfirst[...] = jnp.where(
        lax.broadcasted_iota(jnp.int32, (rmax, block), 0) < ints_ref[2 * held], vt_ref[:, 0:block], 0
    ).astype(BF16)
    pl.semaphore_wait(barrier, n - 1)

    pivot_1, pivot_2, first_1, first_2, column_u = [], [], [], [], []
    for s in range(1, nc):
        cc = lax.rem(c + s, nc)
        copy = remote(pivot_ref, my_piv, piv1_s.at[s], piv1_r.at[s], r, cc)
        copy.start()
        pivot_1.append(copy)
    for s in range(1, nc):
        cc = lax.rem(c + s, nc)
        copy = remote(vfirst, my_vc, v1_s.at[s], v1_r.at[s], r, cc)
        pl.when(r == 0)(copy.start)
        first_1.append(copy)

    masks = []
    m = nc // 2
    while m:
        masks.append(m)
        m //= 2
    u_copies, stages, sem, paths = [], [], 0, [[]]
    for m in masks:
        stages.append([(m, path, sem + q) for q, path in enumerate(paths)])
        sem += len(paths)
        paths = paths + [path + [m] for path in paths]

    def start_stage(entries):
        for m, path, q in entries:
            origin = c
            for step in path:
                origin = origin + step - 2 * step * lax.rem(c // step, 2)
            source = ug.at[origin] if path else ut_ref
            copy = remote(source, ug.at[origin], u_s.at[q], u_r.at[q], r, flip(m))
            copy.start()
            u_copies.append(copy)

    start_stage(stages[0])

    lane = lax.broadcasted_iota(jnp.int32, (1, 128), 1)

    def pack_for(s):
        rr, cc = peer(s)
        target = rr * nc + cc

        def look(j, carry):
            count, found = carry[0], carry[1:]
            hit = ints_ref[j] == target
            found = [jnp.where(hit & (count == k), j, found[k]) for k in range(cap)]
            return (jnp.where(hit, count + 1, count), *found)

        count, *found = lax.fori_loop(0, held, look, (jnp.int32(0),) * (cap + 1))
        row = jnp.full((1, 128), -1, jnp.int32)
        for k in range(cap):
            pack[s * cap + k] = contrib_ref[found[k]]
            row = jnp.where(lane == k, jnp.where(count > k, ints_ref[held + found[k]], -1), row)
        labels[s] = row

    mine = arr_ref.at[pl.ds(me * cap, cap)]
    block_copies = []

    def send(s):
        rr, cc = peer(s)
        copies = (
            remote(pack.at[pl.ds(s * cap, cap)], mine, blk_s.at[s], blk_r.at[s], rr, cc),
            remote(labels.at[s], lab_ref.at[me], lab_s.at[s], lab_r.at[s], rr, cc),
        )
        for copy in copies:
            copy.start()
            block_copies.append(copy)

    far = [s for s in range(1, n) if s % nc >= wing]
    near = [s for s in range(1, n) if s % nc < wing]
    order = [s for pair in zip(far, near + [0]) for s in pair if s]
    early = order[: (EARLY * len(order)) // 16]
    late = order[len(early) :]
    ahead = early[: nc // 2]
    for s in ahead:
        pack_for(s)

    for copy in pivot_1:
        copy.wait_recv()
    for s in range(1, nr):
        rr = lax.rem(r + s, nr)
        copy = remote(row_piv, row_piv, piv2_s.at[s], piv2_r.at[s], rr, c)
        copy.start()
        pivot_2.append(copy)

    @pl.when(r == 0)
    def _():
        vc[pl.ds(pl.multiple_of(c * rmax, rmax), rmax)] = vfirst[...]
        for copy in first_1:
            copy.wait_recv()

    for s in range(1, nr):
        rr = lax.rem(r + s, nr)
        copy = remote(vc, vc, v2_s.at[s], v2_r.at[s], rr, c)
        pl.when(r == 0)(copy.start)
        first_2.append((s, copy))
        copy = remote(first_u, uc, uc_s.at[s], uc_r.at[s], rr, c)
        pl.when(r == 0)(copy.start)
        column_u.append((s, copy))

    for s in ahead:
        send(s)
    for s in early[len(ahead) :]:
        pack_for(s)
        send(s)
    for s in late + [0]:
        pack_for(s)
    own = [
        pltpu.make_async_copy(pack.at[pl.ds(0, cap)], mine, loc.at[2]),
        pltpu.make_async_copy(labels.at[0], lab_ref.at[me], loc.at[3]),
    ]
    for copy in own:
        copy.start()

    for copy in pivot_2:
        copy.wait_recv()

    work1[...] = piv[0:half, 0:half]
    inverse_factor(work1)
    inv1 = work1[...]
    low = exact_dot(piv[half:, 0:half], inv1, ((1,), (1,)))
    work2[...] = piv[half:, half:] - exact_dot(low, low, ((1,), (1,)))

    sent = 0
    for entries in stages[1:]:
        for copy in u_copies[sent:]:
            copy.wait_recv()
        sent = len(u_copies)
        start_stage(entries)

    inverse_factor(work2)
    inv2 = work2[...]
    inv21 = -exact_dot(inv2, exact_dot(low, inv1, ((1,), (0,))), ((1,), (0,)))
    inverse = jnp.concatenate(
        [
            jnp.concatenate([inv1, jnp.zeros_like(inv1)], axis=1),
            jnp.concatenate([inv21, inv2], axis=1),
        ],
        axis=0,
    )
    parts = split3(inverse)
    place = lax.broadcasted_iota(jnp.int32, (rmax, block), 0)
    masked = [
        jnp.where(place < ints_ref[2 * held + i], vt_ref[:, i * block : (i + 1) * block], 0).astype(BF16)
        for i in range(per_dev)
    ]
    g_own = solve(parts, jnp.concatenate(masked, axis=0))

    for s, copy in first_2:
        pl.when(r == 0)(copy.wait_send)
        pl.when(lax.rem(r + nr - s, nr) == 0)(copy.wait_recv)
    g_columns = solve(parts, vc[...])
    mid_out[...] = lax.dot_general(
        g_columns, g_own, (((1,), (1,)), ((), ())), preferred_element_type=F32
    ).astype(BF16)
    mid_copies = []
    for s in range(1, nc):
        cc = lax.rem(c + s, nc)
        rows = mid_out.at[pl.ds(pl.multiple_of(cc * rmax, rmax), rmax)]
        copy = remote(rows, mid_in.at[c], mid_s.at[s], mid_r.at[s], r, cc)
        copy.start()
        mid_copies.append(copy)
    for s in late:
        send(s)
    mid_in[c] = mid_out[pl.ds(pl.multiple_of(c * rmax, rmax), rmax)]

    load_u.wait()
    pl.when(r == 0)(load_uc.wait)
    for s, copy in column_u:
        pl.when(r == 0)(copy.wait_send)
        pl.when(lax.rem(r + nr - s, nr) == 0)(copy.wait_recv)
    for copy in u_copies[:sent]:
        copy.wait_send()
    for copy in u_copies[sent:]:
        copy.wait()
    for copy in mid_copies:
        copy.wait()

    right = uc[...]

    def update(q, carry):
        for i in range(per_dev):
            left = jnp.dot(
                mid_in[q, :, i * rmax : (i + 1) * rmax],
                ug[q, :, i * block : (i + 1) * block],
                preferred_element_type=F32,
            ).astype(BF16)
            rows = pl.ds(pl.multiple_of((q * per_dev + i) * block, block), block)
            term_ref[rows] = lax.dot_general(
                left, right, (((0,), (0,)), ((), ())), preferred_element_type=F32
            )
        return carry

    lax.fori_loop(0, nc, update, 0)

    for copy in pivot_1 + pivot_2:
        copy.wait_send()

    @pl.when(r == 0)
    def _():
        for copy in first_1:
            copy.wait_send()

    for copy in own:
        copy.wait()
    for copy in block_copies:
        copy.wait()


def add_kernel(cap, lab_ref, parent_ref, term_ref, arr_ref, out_ref, total, head, nxt, done):
    slots, block, _ = arr_ref.shape
    places = head.shape[0]

    def clear(i, carry):
        head[i] = -1
        return carry

    def link(j, carry):
        label = lab_ref[j // cap, 0, lax.rem(j, cap)]

        @pl.when(label >= 0)
        def _():
            nxt[j] = head[label]
            head[label] = j

        return carry

    lax.fori_loop(0, places, clear, 0)
    lax.fori_loop(0, slots, link, 0)

    def each(i, carry):
        rows = pl.ds(pl.multiple_of(i * block, block), block)
        first = head[i]

        @pl.when(first < 0)
        def _():
            total[rows] = parent_ref[rows].astype(F32) - term_ref[rows]

        @pl.when(first >= 0)
        def _():
            total[rows] = parent_ref[rows].astype(F32) + arr_ref[first].astype(F32) - term_ref[rows]

            def add(j):
                total[rows] += arr_ref[j].astype(F32)
                return nxt[j]

            lax.while_loop(lambda j: j >= 0, add, nxt[first])

        pltpu.make_async_copy(total.at[rows], out_ref.at[rows], done.at[i]).start()

        return carry

    lax.fori_loop(0, places, each, 0)

    def finish(i, carry):
        rows = pl.ds(pl.multiple_of(i * block, block), block)
        pltpu.make_async_copy(total.at[rows], out_ref.at[rows], done.at[i]).wait()
        return carry

    lax.fori_loop(0, places, finish, 0)


def on_device(parent, contrib, owner, slot, pivot, u_factor, v_factor, rank):
    nr = lax.axis_size("row")
    nc = lax.axis_size("col")
    n = nr * nc
    held, block, _ = contrib.shape
    cap = max(2, (held + n - 1) // n)
    rmax = u_factor.shape[1]
    per_dev = rank.shape[0]
    half = block // 2
    slots = n * cap

    dma = pltpu.SemaphoreType.DMA
    vmem = pl.BlockSpec(memory_space=pltpu.VMEM)
    smem = pl.BlockSpec(memory_space=pltpu.SMEM)
    anywhere = pl.BlockSpec(memory_space=pl.ANY)
    arrived, in_labels, term = pl.pallas_call(
        functools.partial(exchange_kernel, nr, nc, cap, per_dev),
        out_shape=(
            jax.ShapeDtypeStruct((slots, block, block), contrib.dtype),
            jax.ShapeDtypeStruct((n, 1, 128), jnp.int32),
            jax.ShapeDtypeStruct(parent.shape, F32),
        ),
        in_specs=[smem, vmem, vmem, vmem],
        out_specs=(anywhere, anywhere, vmem),
        scratch_shapes=[
            pltpu.VMEM((slots, block, block), contrib.dtype),
            pltpu.VMEM((block, block), F32),
            pltpu.VMEM((rmax, block), BF16),
            pltpu.VMEM((nc * rmax, block), BF16),
            pltpu.VMEM((nc, rmax, per_dev * block), BF16),
            pltpu.VMEM((rmax, block), BF16),
            pltpu.VMEM((nc * rmax, per_dev * rmax), BF16),
            pltpu.VMEM((nc, rmax, per_dev * rmax), BF16),
            pltpu.VMEM((n, 1, 128), jnp.int32),
            pltpu.VMEM((half, half), F32),
            pltpu.VMEM((half, half), F32),
        ]
        + [dma((n,))] * 4
        + [dma((nc,))] * 8
        + [dma((nr,))] * 6
        + [dma((5,))],
        compiler_params=pltpu.CompilerParams(
            collective_id=0, has_side_effects=True, vmem_limit_bytes=28 << 20
        ),
    )(jnp.concatenate([owner[:, 0], slot, rank]), contrib, pivot, jnp.concatenate([v_factor.T, u_factor.T], axis=0))

    places = parent.shape[0] // block
    return pl.pallas_call(
        functools.partial(add_kernel, cap),
        out_shape=jax.ShapeDtypeStruct(parent.shape, F32),
        in_specs=[smem, vmem, vmem, vmem],
        out_specs=anywhere,
        scratch_shapes=[
            pltpu.VMEM(parent.shape, F32),
            pltpu.SMEM((places,), jnp.int32),
            pltpu.SMEM((slots,), jnp.int32),
            dma((places,)),
        ],
        compiler_params=pltpu.CompilerParams(vmem_limit_bytes=24 << 20),
    )(in_labels, parent, term, arrived)


def solution(mesh):
    in_specs = (
        P(("front", "row"), "col"),
        P(("front", "row", "col"), None, None),
        P(("front", "row", "col"), None),
        P(("front", "row", "col")),
        P(("front", "row", "col"), None),
        P(("front", "row", "col"), None),
        P(("front", "row", "col"), None),
        P(("front", "row", "col")),
    )
    return jax.shard_map(
        on_device, mesh=mesh, in_specs=in_specs, out_specs=P(("front", "row"), "col"), check_vma=False
    )
```
